256 devices in a mesh: prow: 32 (over x, z), pcol: 8 (over y, core).
Axes of the slice: x: 4, y: 4, z: 8, core: 2. Of those that a mesh axis runs over, the one named last changes fastest.
Arguments:
- matrix: float32 [2, 8192, 8, 2048], P(None, 'prow', None, 'pcol'), may hold values from -6 to 6
- pattern: int32 [64, 64], replicated, may hold values from 0 to 1, as said below
- row_perm: int32 [2, 8192], P(None, 'prow'), may hold values from 0 to 255, as said below
- lower_inv: float32 [3, 256, 256], replicated, as said below
- upper_inv: float32 [3, 256, 256], replicated, as said below
Outputs:
- factored: float32 [2, 8192, 8, 2048], P(None, 'prow', None, 'pcol')
The draws below stay inside these ranges and needn't reach their ends.
Inputs may be any that keep to these rules, and one draw needn't show every extreme that they name: `pattern`: 1 where a block is kept, 0 where it is dropped; every diagonal entry is 1. `row_perm`: each aligned group of 256 entries is a permutation of 0 to 255, the source row within the same block row. `lower_inv`: lower triangular with ones on the diagonal. `upper_inv`: upper triangular with nonzero diagonal.
All inputs are finite; a program needn't handle non-finite values.
Results may differ from the reference program's by a relative error of at most 0.0001.
Values sent between devices are 32-bit elements; how exact they have to be, the bound alone decides.
No kernel may reach another device: no remote copies, remote signals or barrier semaphores. Data moves between devices by JAX's collectives and lax.ppermute only.
A program may use at most 64 MiB of HBM per device.

```python
import math
import jax
import jax.numpy as jnp
from jax import lax

BLOCK = 256
PANELS = 3
ROW_BLOCKS = 2
COL_BLOCKS = 8
N_PROW = 32
N_PCOL = 8


def draw_pattern(key, part):
    key = jax.random.fold_in(key, 1)
    nblocks = ROW_BLOCKS * N_PROW
    density = jax.random.randint(jax.random.fold_in(key, 11), (nblocks, 1), 300, 1001)
    coins = jax.random.randint(jax.random.fold_in(key, 12), (nblocks, nblocks), 0, 1000)
    rows = lax.broadcasted_iota(jnp.int32, (nblocks, nblocks), 0)
    cols = lax.broadcasted_iota(jnp.int32, (nblocks, nblocks), 1)
    kept = jnp.logical_or(coins < density, rows == cols)
    return kept.astype(jnp.int32)


def draw_row_perm(key, part):
    key = jax.random.fold_in(key, 2)
    nblocks = ROW_BLOCKS * N_PROW
    keys = jax.random.split(key, nblocks)
    perms = jax.vmap(lambda single: jax.random.permutation(single, BLOCK))(keys)
    return perms.reshape(ROW_BLOCKS, N_PROW * BLOCK).astype(jnp.int32)


def draw_lower_inv(key, part):
    key = jax.random.fold_in(key, 3)
    shape = (PANELS, BLOCK, BLOCK)
    rows = lax.broadcasted_iota(jnp.int32, shape, 1)
    cols = lax.broadcasted_iota(jnp.int32, shape, 2)
    spread = 0.6 / math.sqrt(BLOCK)
    off = jax.random.normal(key, shape, jnp.float32) * spread
    ones = jnp.where(rows == cols, 1.0, 0.0).astype(jnp.float32)
    return jnp.where(rows > cols, off, ones).astype(jnp.float32)


def draw_upper_inv(key, part):
    key = jax.random.fold_in(key, 4)
    shape = (PANELS, BLOCK, BLOCK)
    rows = lax.broadcasted_iota(jnp.int32, shape, 1)
    cols = lax.broadcasted_iota(jnp.int32, shape, 2)
    spread = 0.6 / math.sqrt(BLOCK)
    off = jax.random.normal(jax.random.fold_in(key, 5), shape, jnp.float32) * spread
    diag = jnp.exp(jax.random.uniform(jax.random.fold_in(key, 6), shape, jnp.float32, -0.4, 0.4))
    upper = jnp.where(rows < cols, off, jnp.where(rows == cols, diag, 0.0))
    return (upper / 16.0).astype(jnp.float32)


def steps_of(rng, extent, cuts, low, high):
    factor_of, own = 1.0, jax.random.fold_in(rng, 6)
    for position, parts in cuts:
        draws = jnp.exp(jax.random.uniform(jax.random.fold_in(own, position), (parts,), jnp.float32, low / len(cuts), high / len(cuts)))
        factor_of = factor_of * jnp.repeat(draws, extent[position] // parts).reshape([-1 if axis == position else 1 for axis in range(len(extent))])
    return factor_of


def gaussian(key, extent, scale, reach, cuts=(), kind=jnp.bfloat16):
    values = jax.random.normal(key, extent, jnp.float32) * scale
    if len(cuts) > 0:
        values = steps_of(key, extent, cuts, -0.22, 0.18) * values
    return jnp.clip(values, min=-reach, max=reach).astype(kind)


def setup_inputs(seed: int = 0) -> dict:
    arg_keys = jax.random.split(jax.random.key(seed), 6)
    return {
        "matrix": gaussian(arg_keys[0], (ROW_BLOCKS, N_PROW * BLOCK, COL_BLOCKS, N_PCOL * BLOCK), 1.0, 6.0, ((1, 32), (3, 8)), jnp.float32),
        "pattern": draw_pattern(jax.random.fold_in(arg_keys[5], 71), 0),
        "row_perm": draw_row_perm(jax.random.fold_in(arg_keys[5], 71), 0),
        "lower_inv": draw_lower_inv(jax.random.fold_in(arg_keys[5], 71), 0),
        "upper_inv": draw_upper_inv(jax.random.fold_in(arg_keys[5], 71), 0),
    }


def reference(matrix, pattern, row_perm, lower_inv, upper_inv):
    nblocks = ROW_BLOCKS * N_PROW
    high = lax.Precision.HIGHEST
    blocks = matrix.reshape(nblocks, BLOCK, nblocks, BLOCK)
    order = row_perm.reshape(nblocks, BLOCK)
    blocks = jax.vmap(lambda single, rows: single[rows])(blocks, order)
    maskf = pattern.astype(jnp.float32)
    blocks = blocks * maskf[:, None, :, None]
    every = jnp.arange(nblocks, dtype=jnp.int32)
    for step in range(PANELS):
        column = blocks[:, :, step, :]
        lpanel = jnp.einsum('irt,ts->irs', column, upper_inv[step], precision=high)
        upanel = jnp.einsum('rt,tjs->rjs', lower_inv[step], blocks[step], precision=high)
        live_rows = every > step
        live_cols = every > step
        weight = maskf * live_rows[:, None].astype(jnp.float32) * live_cols[None, :].astype(jnp.float32)

        def one_row(items):
            left_block, weight_row, block_row = items
            update = jnp.einsum('rt,tjs->rjs', left_block, upanel, precision=high)
            return block_row - weight_row[None, :, None] * update

        blocks = lax.map(one_row, (lpanel, weight, blocks))
        blocks = blocks.at[:, :, step, :].set(jnp.where(live_rows[:, None, None], lpanel, blocks[:, :, step, :]))
        blocks = blocks.at[step].set(jnp.where(live_cols[None, :, None], upanel, blocks[step]))
    return blocks.reshape(ROW_BLOCKS, N_PROW * BLOCK, nblocks // N_PCOL, N_PCOL * BLOCK)
```

```python
import functools

import jax
import jax.numpy as jnp
from jax import lax
from jax.experimental import pallas as pl
from jax.experimental.pallas import tpu as pltpu

PANELS = 3
NX, NZ = 4, 8
SMEM = pltpu.SMEM
VMEM = pltpu.VMEM
F32 = jnp.float32
BF16 = jnp.bfloat16


def split(value):
    high = value.astype(BF16)
    return high, (value - high.astype(F32)).astype(BF16)


def dot3(a, b):
    (ah, al), (bh, bl) = a, b
    one = functools.partial(jnp.dot, preferred_element_type=F32)
    return one(ah, bh) + (one(ah, bl) + one(al, bh))


def params(mib=48):
    return pltpu.CompilerParams(vmem_limit_bytes=mib * 2**20)


def pack_body(m, quarters, where_ref, pattern_ref, perm_ref, a_ref, *rest):
    out_refs, moved = rest[:-1], rest[-1]
    prow, pcol, turn = where_ref[0], where_ref[1], where_ref[2]
    rows = a_ref.shape[1]
    cols = a_ref.shape[2]

    def move(r, carry):
        for u in range(8):
            moved[r * 8 + u] = a_ref[0, perm_ref[m, r * 8 + u]]
        return carry

    lax.fori_loop(0, rows // 8, move, 0)
    for c in range(cols):
        keep = pattern_ref[m * 32 + prow, c * 8 + pcol].astype(F32)
        block = moved[:, c, :] * keep
        if quarters:
            out_refs[0][c] = block
            part = rows // 4
            for slot in range(4):
                first = lax.rem(turn + slot, 4) * part
                piece = moved[pl.ds(first, part), c, :] * keep
                for h in range(2):
                    out_refs[1][slot, h, c] = piece[h * (part // 2) : (h + 1) * (part // 2)]
        else:
            out_refs[0][c] = block


def pack(m, quarters, where, pattern, perm, matrix):
    _, rows, cols, width = matrix.shape
    half = width // 2
    shapes = [jax.ShapeDtypeStruct((cols, rows, width), F32)]
    specs = [pl.BlockSpec((cols, rows, half), lambda i: (0, 0, i))]
    if quarters:
        shapes.append(jax.ShapeDtypeStruct((4, 2, cols, rows // 8, width), F32))
        specs.append(pl.BlockSpec((4, 2, cols, rows // 8, half), lambda i: (0, 0, 0, 0, i)))
    return pl.pallas_call(
        functools.partial(pack_body, m, quarters),
        grid=(2,),
        in_specs=[
            pl.BlockSpec(memory_space=SMEM),
            pl.BlockSpec(memory_space=SMEM),
            pl.BlockSpec(memory_space=SMEM),
            pl.BlockSpec((1, rows, cols, half), lambda i: (m, 0, 0, i)),
        ],
        out_specs=specs,
        out_shape=shapes,
        scratch_shapes=[VMEM((rows, cols, half), F32)],
        compiler_params=params(),
        name="pack",
    )(where, pattern, perm, matrix)


def left_body(
    where_ref, pattern_ref, cols_ref, corner_ref, linv_ref, uinv_ref,
    lh_ref, ll_ref, ch_ref, cl_ref, raw_ref, both,
):
    prow = where_ref[0]
    turn = where_ref[2]
    part = 64
    for q in range(3):
        for slot in range(4):
            shift = (0, 3, 1, 2)[slot]
            first = lax.rem(turn + shift, 4) * part
            for h in range(2):
                for row in range(2):
                    both[q, row, pl.ds(first + h * 32, 32), :] = corner_ref[q, slot, h, row]
    li = [split(linv_ref[k]) for k in range(2)]
    ui = [split(uinv_ref[k]) for k in range(3)]
    a10, a20 = both[0, 0], both[0, 1]
    a01, a21 = both[1, 0], both[1, 1]
    a02, a12 = both[2, 0], both[2, 1]
    u01 = split(dot3(li[0], split(a01)))
    u02 = split(dot3(li[0], split(a02)))
    l10 = split(dot3(split(a10), ui[0]))
    l20 = split(dot3(split(a20), ui[0]))
    p12 = pattern_ref[1, 2].astype(F32)
    p21 = pattern_ref[2, 1].astype(F32)
    u12 = split(dot3(li[1], split(a12 - p12 * dot3(l10, u02))))
    l21 = split(dot3(split(a21 - p21 * dot3(l20, u01)), ui[1]))
    for n, value in enumerate((l10, l20, l21)):
        ch_ref[n] = value[0]
        cl_ref[n] = value[1]
    for m in range(2):
        row = m * 32 + prow
        rows = pl.ds(m * 256, 256)
        l0 = dot3(split(cols_ref[0, m]), ui[0])
        l0s = split(l0)
        p1 = pattern_ref[row, 1].astype(F32)
        l1 = dot3(split(cols_ref[1, m] - p1 * dot3(l0s, u01)), ui[1])
        l1s = split(l1)
        p2 = pattern_ref[row, 2].astype(F32)
        l2 = dot3(
            split(cols_ref[2, m] - p2 * (dot3(l0s, u02) + dot3(l1s, u12))), ui[2]
        )
        for k, value in enumerate((l0, l1, l2)):
            raw_ref[k, m] = value
            live = jnp.where(row > k, value, 0.0)
            high, low = split(live)
            lh_ref[rows, pl.ds(k * 256, 256)] = high
            ll_ref[rows, pl.ds(k * 256, 256)] = low


def left(where, pattern, cols, corner, lower_inv, upper_inv):
    smem = pl.BlockSpec(memory_space=SMEM)
    vmem = pl.BlockSpec(memory_space=VMEM)
    return pl.pallas_call(
        left_body,
        in_specs=[smem, smem, vmem, vmem, vmem, vmem],
        out_specs=[vmem] * 5,
        out_shape=[
            jax.ShapeDtypeStruct((512, 768), BF16),
            jax.ShapeDtypeStruct((512, 768), BF16),
            jax.ShapeDtypeStruct((3, 256, 256), BF16),
            jax.ShapeDtypeStruct((3, 256, 256), BF16),
            jax.ShapeDtypeStruct((3, 2, 256, 256), F32),
        ],
        scratch_shapes=[VMEM((3, 2, 256, 256), F32)],
        compiler_params=params(),
        name="left",
    )(where, pattern, cols, corner, lower_inv, upper_inv)


def finish_body(
    where_ref, pattern_ref, ap0_ref, ap1_ref, lh_ref, ll_ref, ch_ref, cl_ref, raw_ref, linv_ref,
    *rest,
):
    first_refs, main_refs = rest[0:4], rest[4:12]
    out_ref, panel, upper = rest[12:]
    c = pl.program_id(0)
    prow, pcol, turn = where_ref[0], where_ref[1], where_ref[2]
    col = c * 8 + pcol
    shifts = (0, 3, 1, 2)

    @pl.when(c == 0)
    def _():
        for slot in range(4):
            first = lax.rem(turn + shifts[slot], 4) * 64
            for h in range(2):
                panel[:, pl.ds(first + h * 32, 32), :] = first_refs[slot][h]

    @pl.when(c > 0)
    def _():
        for slot in range(4):
            first = lax.rem(turn + shifts[slot], 4) * 64
            for h in range(2):
                panel[:, pl.ds(first + h * 32, 32), :] = main_refs[slot * 2 + h][:, 0]

    corner = [(ch_ref[n], cl_ref[n]) for n in range(3)]
    li = [split(linv_ref[k]) for k in range(3)]
    u0 = dot3(li[0], split(panel[0]))
    u0s = split(u0)
    p1 = pattern_ref[1, col].astype(F32)
    u1 = dot3(li[1], split(panel[1] - p1 * dot3(corner[0], u0s)))
    u1s = split(u1)
    p2 = pattern_ref[2, col].astype(F32)
    u2 = dot3(li[2], split(panel[2] - p2 * (dot3(corner[1], u0s) + dot3(corner[2], u1s))))
    u2s = split(u2)
    for k, value in enumerate((u0, u1, u2)):
        upper[k] = value
    uh = jnp.concatenate([u0s[0], u1s[0], u2s[0]], axis=0)
    ul = jnp.concatenate([u0s[1], u1s[1], u2s[1]], axis=0)
    total = dot3((lh_ref[...], ll_ref[...]), (uh, ul))
    for m, ap_ref in enumerate((ap0_ref, ap1_ref)):
        row = m * 32 + prow
        keep = pattern_ref[row, col].astype(F32)
        out_ref[m, :, c, :] = ap_ref[0] - keep * total[m * 256 : (m + 1) * 256]

        @pl.when(jnp.logical_and(col < 3, row > col))
        def _():
            out_ref[m, :, c, :] = raw_ref[jnp.minimum(col, 2), m]

        if m == 0:

            @pl.when(jnp.logical_and(row < 3, row < col))
            def _():
                out_ref[m, :, c, :] = upper[jnp.minimum(row, 2)]


def finish(where, pattern, ap0, ap1, lh, ll, ch, cl, raw, lower_inv, firsts, mains):
    smem = pl.BlockSpec(memory_space=SMEM)
    vmem = pl.BlockSpec(memory_space=VMEM)
    block = pl.BlockSpec((1, 256, 256), lambda c: (c, 0, 0))
    main = pl.BlockSpec((3, 1, 32, 256), lambda c: (0, jnp.maximum(c, 1) - 1, 0, 0))
    return pl.pallas_call(
        finish_body,
        grid=(8,),
        in_specs=[smem, smem, block, block] + [vmem] * 6 + [vmem] * 4 + [main] * 8,
        out_specs=pl.BlockSpec((2, 256, 8, 256), lambda c: (0, 0, 0, 0)),
        out_shape=jax.ShapeDtypeStruct((2, 256, 8, 256), F32),
        scratch_shapes=[VMEM((3, 256, 256), F32), VMEM((3, 256, 256), F32)],
        compiler_params=params(),
        name="finish",
    )(where, pattern, ap0, ap1, lh, ll, ch, cl, raw, lower_inv, *firsts, *mains)


def hop(array, step, sources):
    pairs = []
    for x in range(NX):
        for z in range(NZ):
            if sources(x, z):
                to = ((x + step[0]) % NX) * NZ + (z + step[1]) % NZ
                pairs.append((x * NZ + z, to))
    return lax.ppermute(array, "prow", pairs)


def on_device(matrix, pattern, row_perm, lower_inv, upper_inv):
    prow = lax.axis_index("prow")
    pcol = lax.axis_index("pcol")
    x, z = prow // NZ, prow % NZ
    turn = lax.rem(x + 2 * z, 4)
    where = jnp.stack([prow, pcol, turn]).astype(jnp.int32)
    ap0, cut = pack(0, True, where, pattern, row_perm, matrix)
    sent = [hop(cut[d], (d, 0), lambda x, z: x == 0 and z < 3) for d in (1, 3, 2)]
    (ap1,) = pack(1, False, where, pattern, row_perm, matrix)
    columns = lax.all_gather(jnp.stack([ap0[0], ap1[0]]), "pcol", axis=0)
    own = jnp.where(x == 0, cut[0], sent[0] + sent[1] + sent[2])
    far = hop(own, (0, 4), lambda x, z: z < 3)
    held = jnp.where(z < 4, own, far)
    some = lambda x, z: z % 4 < 3
    after = hop(held, (2, 1), some)
    before = hop(held, (2, -1), some)
    two = hop(held, (0, 2), some)
    phase = z % 4

    def row(r, part):
        return jnp.where(
            phase == r, held[part], jnp.where(phase == (r + 1) % 4, after[part], jnp.where(phase == (r + 3) % 4, before[part], two[part]))
        )

    every = lambda x, z: True
    start = jnp.stack([jnp.stack([row(r, (h, 0)) for r in range(3)]) for h in range(2)])
    mine = [jnp.stack([row(r, (h, slice(1, None))) for r in range(3)]) for h in range(2)]
    firsts = [
        start,
        hop(start, (1, 0), every),
        hop(start, (-1, 0), every),
        hop(start, (0, 1), every),
    ]
    low = [jnp.where(pcol == 0, f[:, 1], f[:, 0]) for f in firsts]
    high = [jnp.where(pcol == 2, f[:, 1], f[:, 2]) for f in firsts]
    corner = jnp.stack([jnp.stack([a, b], axis=1) for a, b in zip(low, high)])
    corner = lax.all_gather(corner, "pcol", axis=0)[:3]
    mains = [mine[0], mine[1]]
    mains += [hop(mine[0], (1, 0), every), hop(mine[1], (1, 0), every)]
    mains += [hop(mine[0], (-1, 0), every), hop(mine[1], (-1, 0), every)]
    mains += [hop(mine[0], (0, 1), every), hop(mine[1], (0, -1), every)]
    lh, ll, ch, cl, raw = left(where, pattern, columns[:3], corner, lower_inv, upper_inv)
    return finish(where, pattern, ap0, ap1, lh, ll, ch, cl, raw, lower_inv, firsts, mains)


def solution(mesh):
    P = jax.sharding.PartitionSpec
    in_specs = (P(None, "prow", None, "pcol"), P(), P(None, "prow"), P(), P())
    out_specs = P(None, "prow", None, "pcol")
    return jax.shard_map(
        on_device, mesh=mesh, in_specs=in_specs, out_specs=out_specs, check_vma=False
    )
```

```python
import functools

import jax
import jax.numpy as jnp
from jax import lax
from jax.experimental import pallas as pl
from jax.experimental.pallas import tpu as pltpu

NX, NZ = 4, 8
SHIFTS = (0, 3, 1, 2)
SMEM = pl.BlockSpec(memory_space=pltpu.SMEM)
ANY = pl.BlockSpec(memory_space=pl.ANY)
HERE = pl.BlockSpec(memory_space=pltpu.VMEM)
VMEM = pltpu.VMEM
F32 = jnp.float32
BF16 = jnp.bfloat16
shaped = jax.ShapeDtypeStruct


def params(mib):
    return pltpu.CompilerParams(vmem_limit_bytes=mib * 2**20)


def split(value):
    high = value.astype(BF16)
    return high, (value - high.astype(F32)).astype(BF16)


def wide(value):
    high, low = split(value)
    return jnp.concatenate([high, high, low], axis=1)


def tall(value):
    high, low = split(value)
    return jnp.concatenate([high, low, high], axis=0)


def dot(a, b):
    return jnp.dot(a, b, preferred_element_type=F32)


def gather_rows(m, perm_ref, source, moved):
    def move(r, carry):
        for u in range(16):
            moved[r * 16 + u] = source[perm_ref[m, r * 16 + u]]
        return carry

    lax.fori_loop(0, 16, move, 0)


def block_of(m, c, where_ref, pattern_ref, moved):
    keep = pattern_ref[m * 32 + where_ref[0], c * 8 + where_ref[1]].astype(F32)
    return moved[:, c, :] * keep


def pack_first_body(
    where_ref, pattern_ref, perm_ref, a_ref, faces_ref, m0, m1, m2, m3, raw, moved, packed, sem,
):
    loads = [
        pltpu.make_async_copy(
            a_ref.at[m, pl.ds(n * 64, 64)], raw.at[m, pl.ds(n * 64, 64)], sem.at[m * 4 + n]
        )
        for m in range(2)
        for n in range(4)
    ]
    for load in loads:
        load.start()
    for load in loads[:4]:
        load.wait()
    gather_rows(0, perm_ref, raw.at[0], moved)
    copies = []

    def copy(source, target):
        one = pltpu.make_async_copy(source, target, sem.at[8 + len(copies)])
        one.start()
        copies.append(one)

    def face(m, block):
        for j in range(8):
            copy(packed.at[block, pl.ds(j * 32, 32)], faces_ref.at[j, m])

    mains = (m0, m1, m2, m3)
    turn = where_ref[2]
    starts = [pl.multiple_of(lax.rem(turn + slot, 4) * 64, 64) for slot in range(4)]
    for c in range(8):
        packed[c] = block_of(0, c, where_ref, pattern_ref, moved)
        if c == 0:
            face(0, 0)
        if c % 4 == 3:
            part = pl.ds(c - 3, 4)
            for slot in (2, 1, 3, 0):
                for h in range(2):
                    rows = pl.ds(starts[slot] + h * 32, 32)
                    copy(packed.at[part, rows], mains[slot].at[h, part])
    for load in loads[4:]:
        load.wait()
    gather_rows(1, perm_ref, raw.at[1], moved)
    packed[8] = block_of(1, 0, where_ref, pattern_ref, moved)
    face(1, 8)
    for one in copies:
        one.wait()


def pack_first(where, pattern, perm, matrix):
    return pl.pallas_call(
        pack_first_body,
        in_specs=[SMEM, SMEM, SMEM, ANY],
        out_specs=[ANY] * 5,
        out_shape=[shaped((8, 2, 32, 256), F32)] + [shaped((2, 8, 32, 256), F32)] * 4,
        scratch_shapes=[
            VMEM((2, 256, 8, 256), F32),
            VMEM((256, 8, 256), F32),
            VMEM((9, 256, 256), F32),
            pltpu.SemaphoreType.DMA((40,)),
        ],
        compiler_params=params(58),
        name="pack_first",
    )(where, pattern, perm, matrix)


def pack_body(where_ref, pattern_ref, perm_ref, a_ref, after_ref, out0_ref, out1_ref, moved):
    for m, out_ref in enumerate((out0_ref, out1_ref)):
        gather_rows(m, perm_ref, a_ref.at[m], moved)
        for c in range(8):
            out_ref[c] = block_of(m, c, where_ref, pattern_ref, moved)


def pack(where, pattern, perm, matrix, after):
    return pl.pallas_call(
        pack_body,
        in_specs=[SMEM, SMEM, SMEM, HERE, ANY],
        out_specs=[HERE, HERE],
        out_shape=[shaped((8, 256, 256), F32)] * 2,
        scratch_shapes=[VMEM((256, 8, 256), F32)],
        compiler_params=params(20),
        name="pack",
    )(where, pattern, perm, matrix, after)


def merge_body(
    found_ref, columns_ref, held0, held1, after, before, two0, two1,
    all_ref, half0, half1, corner_ref, slices, sem,
):
    eight = pl.ds(0, 8)
    waits = []
    for r in range(3):
        for h in range(2):
            n = (r * 2 + h) * 3
            found = found_ref[r * 2 + h]
            sources = ((held0, held1)[h], after.at[h], before.at[h], (two0, two1)[h])

            def copies(source, n=n, r=r, h=h):
                return [
                    pltpu.make_async_copy(source.at[8], slices.at[r, h], sem.at[n]),
                    pltpu.make_async_copy(source.at[eight], all_ref.at[h, r], sem.at[n + 1]),
                    pltpu.make_async_copy(source.at[eight], (half0, half1)[h].at[r], sem.at[n + 2]),
                ]

            for which, source in enumerate(sources):

                @pl.when(found == which)
                def _():
                    for one in copies(source):
                        one.start()

            waits.append(copies(sources[0]))
    for group in waits:
        group[0].wait()
    last = [
        pltpu.make_async_copy(slices, corner_ref.at[q], sem.at[18 + q]) for q in range(8)
    ]
    for one in last:
        one.start()
    for group in waits:
        group[1].wait()
        group[2].wait()
    for one in last:
        one.wait()


def merge(found, columns, *parts):
    half = shaped((3, 8, 32, 256), F32)
    return pl.pallas_call(
        merge_body,
        in_specs=[SMEM] + [ANY] * 7,
        out_specs=[ANY] * 4,
        out_shape=[
            shaped((2, 3, 8, 32, 256), F32), half, half, shaped((8, 3, 2, 32, 256), F32)
        ],
        scratch_shapes=[VMEM((3, 2, 32, 256), F32), pltpu.SemaphoreType.DMA((26,))],
        compiler_params=params(8),
        name="merge",
    )(found, columns, *parts)


def left_body(
    where_ref, pattern_ref, columns_ref, corner_ref, linv_ref, uinv_ref,
    ll_ref, c3_ref, li_ref, raw_ref, column, both, linv, uinv, sem,
):
    prow = where_ref[0]
    copies = [
        pltpu.make_async_copy(linv_ref, linv, sem.at[0]),
        pltpu.make_async_copy(uinv_ref, uinv, sem.at[1]),
    ]
    for q in range(8):
        rows = pl.ds(q * 32, 32)
        copies.append(pltpu.make_async_copy(corner_ref.at[q], both.at[:, :, rows], sem.at[2 + q]))
        copies.append(pltpu.make_async_copy(columns_ref.at[q], column.at[:, :, rows], sem.at[10 + q]))
    for one in copies:
        one.start()
    for one in copies:
        one.wait()
    li = [wide(linv[k]) for k in range(3)]
    ui = [tall(uinv[k]) for k in range(3)]
    for k in range(3):
        li_ref[k] = li[k]
    a01, a02 = both[0, 0], both[0, 1]
    a10, a12 = both[1, 0], both[1, 1]
    a20, a21 = both[2, 0], both[2, 1]
    u01 = tall(dot(li[0], tall(a01)))
    u02 = tall(dot(li[0], tall(a02)))
    l10 = wide(dot(wide(a10), ui[0]))
    l20 = wide(dot(wide(a20), ui[0]))
    p12 = pattern_ref[1, 2].astype(F32)
    p21 = pattern_ref[2, 1].astype(F32)
    u12 = tall(dot(li[1], tall(a12 - p12 * dot(l10, u02))))
    l21 = wide(dot(wide(a21 - p21 * dot(l20, u01)), ui[1]))
    for n, value in enumerate((l10, l20, l21)):
        c3_ref[n] = value
    for m in range(2):
        row = m * 32 + prow
        rows = pl.ds(m * 256, 256)
        l0 = dot(wide(column[0, m]), ui[0])
        l0w = wide(l0)
        p1 = pattern_ref[row, 1].astype(F32)
        l1 = dot(wide(column[1, m] - p1 * dot(l0w, u01)), ui[1])
        l1w = wide(l1)
        p2 = pattern_ref[row, 2].astype(F32)
        l2 = dot(wide(column[2, m] - p2 * (dot(l0w, u02) + dot(l1w, u12))), ui[2])
        for k, value in enumerate((l0, l1, l2)):
            raw_ref[k, m] = value
            high, low = split(jnp.where(row > k, value, 0.0))
            ll_ref[rows, pl.ds(k * 768, 256)] = high
            ll_ref[rows, pl.ds(k * 768 + 256, 256)] = high
            ll_ref[rows, pl.ds(k * 768 + 512, 256)] = low


def left(where, pattern, columns, corner, lower_inv, upper_inv):
    outs = [
        shaped((512, 2304), BF16),
        shaped((3, 256, 768), BF16),
        shaped((3, 256, 768), BF16),
        shaped((3, 2, 256, 256), F32),
    ]
    return pl.pallas_call(
        left_body,
        in_specs=[SMEM, SMEM, ANY, ANY, ANY, ANY],
        out_specs=[HERE] * 4,
        out_shape=outs,
        scratch_shapes=[
            VMEM((3, 2, 256, 256), F32),
            VMEM((3, 2, 256, 256), F32),
            VMEM((3, 256, 256), F32),
            VMEM((3, 256, 256), F32),
            pltpu.SemaphoreType.DMA((18,)),
        ],
        compiler_params=params(20),
        name="left",
    )(where, pattern, columns, corner, lower_inv, upper_inv)


RANGES = ((0, 4), (4, 8))


def finish_body(
    where_ref, pattern_ref, ap0, ap1, ll, c3, li, raw, mine, lower, higher, half0, half1,
    out_ref, panel, upper, out, sem,
):
    prow, pcol, turn = where_ref[0], where_ref[1], where_ref[2]
    count = [0]

    def copy(source, target):
        one = pltpu.make_async_copy(source, target, sem.at[count[0]])
        count[0] += 1
        one.start()
        return one

    starts = [pl.multiple_of(lax.rem(turn + s, 4) * 64, 64) for s in SHIFTS]
    halves = [ref.at[h] for ref in (mine, lower, higher) for h in range(2)] + [half0, half1]

    def panels(n):
        lo, hi = RANGES[n]
        part = pl.ds(lo, hi - lo)
        for slot in range(4):
            for h in range(2):
                rows = pl.ds(starts[slot] + h * 32, 32)
                yield copy(halves[slot * 2 + h].at[:, part], panel.at[:, part, rows])

    def wait(group):
        for one in group:
            one.wait()

    def keep(i, c):
        return pattern_ref[i, c * 8 + pcol].astype(F32)

    def keeps(k, group):
        return jnp.concatenate([jnp.full((1, 256), keep(k, c), F32) for c in group], axis=1)

    def block(k, group):
        return jnp.concatenate([panel[k, c] for c in group], axis=1)

    def done(k, group, value):
        for n, c in enumerate(group):
            panel[k, c] = value[:, n * 256 : (n + 1) * 256]
        value = tall(value)
        upper[pl.ds(k * 768, 768), pl.ds(group[0] * 256, len(group) * 256)] = value
        return value

    def stages(group):
        u0 = done(0, group, dot(li[0], tall(block(0, group))))
        yield
        both = dot(c3[pl.ds(0, 2)].reshape(512, 768), u0)
        value = block(1, group) - keeps(1, group) * both[:256]
        u1 = done(1, group, dot(li[1], tall(value)))
        yield
        both = both[256:] + dot(c3[2], u1)
        value = block(2, group) - keeps(2, group) * both
        done(2, group, dot(li[2], tall(value)))
        yield

    def fix(m):
        @pl.when(jnp.logical_and(pcol < 3, m * 32 + prow > pcol))
        def _():
            out[m, :, 0, :] = raw[jnp.minimum(pcol, 2), m]

        if m == 0:

            @pl.when(prow < 3)
            def _():
                mine = jnp.minimum(prow, 2)
                for c in range(8):

                    @pl.when(prow < c * 8 + pcol)
                    def _():
                        out[0, :, c, :] = panel[mine, c]

    def update(c, m):
        total = dot(ll[pl.ds(m * 256, 256), :], upper[:, pl.ds(c * 256, 256)])
        out[m, :, c, :] = (ap0, ap1)[m][c] - keep(m * 32 + prow, c) * total

    groups = [[*panels(n)] for n in range(2)]
    wait(groups[0])
    for _ in stages(range(4)):
        pass
    wait(groups[1])
    for n, _ in enumerate(stages(range(4, 8))):
        if n < 2:
            for c in range(4):
                update(c, n)
    for c in range(4, 8):
        update(c, 0)
    fix(0)
    last = [copy(out.at[0], out_ref.at[0])]
    for c in (4, 5, 6, 7):
        update(c, 1)
    fix(1)
    last.append(copy(out.at[1], out_ref.at[1]))
    wait(last)


def finish(where, pattern, ap0, ap1, ll, c3, li, raw, *mains):
    return pl.pallas_call(
        finish_body,
        in_specs=[SMEM, SMEM] + [HERE] * 6 + [ANY] * 5,
        out_specs=ANY,
        out_shape=shaped((2, 256, 8, 256), F32),
        scratch_shapes=[
            VMEM((3, 8, 256, 256), F32),
            VMEM((2304, 2048), BF16),
            VMEM((2, 256, 8, 256), F32),
            pltpu.SemaphoreType.DMA((48,)),
        ],
        compiler_params=params(32),
        name="finish",
    )(where, pattern, ap0, ap1, ll, c3, li, raw, *mains)


def hop(array, steps, sources=lambda x, z: True):
    pairs = []
    for x in range(NX):
        for z in range(NZ):
            if sources(x, z):
                step = steps[z] if len(steps) > 1 else steps[0]
                to = ((x + step[0]) % NX) * NZ + (z + step[1]) % NZ
                pairs.append((x * NZ + z, to))
    return lax.ppermute(array, "prow", pairs)


def to_all(array):
    count = lax.axis_size("pcol")
    return lax.all_to_all(jnp.broadcast_to(array, (count, *array.shape)), "pcol", 0, 0)


PICK = (
    ((0, 1, 3, 2, 0, 1, 3, 2), (0, 1, 3, 2, 0, 1, 3, 2)),
    ((2, 0, 1, 3, 2, 0, 1, 3), (2, 0, 1, 3, 2, 0, 1, 3)),
    ((3, 2, 0, 1, 3, 2, 0, 1), (1, 2, 0, 1, 3, 3, 2, 0)),
)


def on_device(matrix, pattern, row_perm, lower_inv, upper_inv):
    prow = lax.axis_index("prow")
    pcol = lax.axis_index("pcol")
    x, z = prow // NZ, prow % NZ
    root = lambda x, z: x == 0 and z < 3
    where = jnp.stack([prow, pcol, lax.rem(x + 2 * z, 4)]).astype(jnp.int32)
    faces, *cut = pack_first(where, pattern, row_perm, matrix)
    sent = [hop(cut[d], [(d, 0)], root) for d in (2, 1, 3)]
    faces = lax.all_to_all(faces, "pcol", 0, 0)
    columns = to_all(faces[:3])
    extra = jnp.stack(
        [jnp.where(z == 0, faces[1, 0], faces[0, 0]), jnp.where(z == 2, faces[1, 0], faces[2, 0])]
    )
    extra_sent = [hop(extra, [(d, 0)], root) for d in (2, 1, 3)]
    own = jnp.where(x == 0, cut[0], sum(sent))
    own_extra = jnp.where(x == 0, extra, sum(extra_sent))
    own = jnp.concatenate([own, own_extra[:, None]], axis=1)
    far = [
        hop(own[0], [(0, 4)], lambda x, z: z < 3),
        hop(own[1], [(0, 4), (0, 4), (2, 5)], lambda x, z: z < 3),
    ]
    held = [jnp.where(z < 4, own[h], far[h]) for h in range(2)]
    both = jnp.stack(held)
    after = hop(both, [(2, 1)], lambda x, z: z != 3)
    before = hop(both, [(2, -1)], lambda x, z: z != 3)
    two = [
        hop(held[0], [(0, 2)], lambda x, z: z % 4 < 3),
        hop(
            held[1],
            [(0, -2), (0, -2), (0, 2), None, (0, -2), (0, -2), None, (0, -2)],
            lambda x, z: z not in (3, 6),
        ),
    ]

    found = jnp.array(PICK, jnp.int32)[:, :, z].reshape(6)
    mine, half0, half1, corner = merge(found, columns, held[0], held[1], after, before, two[0], two[1])
    corner = lax.all_to_all(corner, "pcol", 0, 0)
    ap0, ap1 = pack(where, pattern, row_perm, matrix, mine)
    lower, higher = hop(mine, [(1, 0)]), hop(mine, [(-1, 0)])
    half0, half1 = hop(half0, [(0, 1)]), hop(half1, [(0, -1)])
    ll, c3, li, raw = left(where, pattern, columns, corner, lower_inv, upper_inv)
    return finish(where, pattern, ap0, ap1, ll, c3, li, raw, mine, lower, higher, half0, half1)


def solution(mesh):
    P = jax.sharding.PartitionSpec
    in_specs = (P(None, "prow", None, "pcol"), P(), P(None, "prow"), P(), P())
    out_specs = P(None, "prow", None, "pcol")
    return jax.shard_map(
        on_device, mesh=mesh, in_specs=in_specs, out_specs=out_specs, check_vma=False
    )
```

```python
import functools

import jax
import jax.numpy as jnp
from jax import lax
from jax.experimental import pallas as pl
from jax.experimental.pallas import tpu as pltpu

NX, NZ = 4, 8
SHIFTS = (0, 3, 1, 2)
SMEM = pl.BlockSpec(memory_space=pltpu.SMEM)
ANY = pl.BlockSpec(memory_space=pl.ANY)
HERE = pl.BlockSpec(memory_space=pltpu.VMEM)
VMEM = pltpu.VMEM
F32 = jnp.float32
BF16 = jnp.bfloat16
shaped = jax.ShapeDtypeStruct


def params(mib):
    return pltpu.CompilerParams(vmem_limit_bytes=mib * 2**20)


def split(value):
    high = value.astype(BF16)
    return high, (value - high.astype(F32)).astype(BF16)


def wide(value):
    high, low = split(value)
    return jnp.concatenate([high, high, low], axis=1)


def tall(value):
    high, low = split(value)
    return jnp.concatenate([high, low, high], axis=0)


def dot(a, b):
    return jnp.dot(a, b, preferred_element_type=F32)


def gather_rows(m, perm_ref, source, moved):
    def move(r, carry):
        for u in range(16):
            moved[r * 16 + u] = source[perm_ref[m, r * 16 + u]]
        return carry

    lax.fori_loop(0, 16, move, 0)


def block_of(m, c, where_ref, pattern_ref, moved):
    keep = pattern_ref[m * 32 + where_ref[0], c * 8 + where_ref[1]].astype(F32)
    return moved[:, c, :] * keep


def pack_first_body(
    where_ref, pattern_ref, perm_ref, a_ref, faces_ref, m0, m1, m2, m3, raw, moved, packed, sem,
):
    loads = [
        pltpu.make_async_copy(
            a_ref.at[m, pl.ds(n * 64, 64)], raw.at[m, pl.ds(n * 64, 64)], sem.at[m * 4 + n]
        )
        for m in range(2)
        for n in range(4)
    ]
    for load in loads:
        load.start()
    for load in loads[:4]:
        load.wait()
    gather_rows(0, perm_ref, raw.at[0], moved)
    copies = []

    def copy(source, target):
        one = pltpu.make_async_copy(source, target, sem.at[8 + len(copies)])
        one.start()
        copies.append(one)

    def face(m, block):
        for j in range(8):
            copy(packed.at[block, pl.ds(j * 32, 32)], faces_ref.at[j, m])

    mains = (m0, m1, m2, m3)
    turn = where_ref[2]
    starts = [pl.multiple_of(lax.rem(turn + slot, 4) * 64, 64) for slot in range(4)]
    for c in range(8):
        packed[c] = block_of(0, c, where_ref, pattern_ref, moved)
        if c == 0:
            face(0, 0)
        if c % 4 == 3:
            part = pl.ds(c - 3, 4)
            for slot in (2, 1, 3, 0):
                for h in range(2):
                    rows = pl.ds(starts[slot] + h * 32, 32)
                    copy(packed.at[part, rows], mains[slot].at[h, part])
    for load in loads[4:]:
        load.wait()
    gather_rows(1, perm_ref, raw.at[1], moved)
    packed[8] = block_of(1, 0, where_ref, pattern_ref, moved)
    face(1, 8)
    for one in copies:
        one.wait()


def pack_first(where, pattern, perm, matrix):
    return pl.pallas_call(
        pack_first_body,
        in_specs=[SMEM, SMEM, SMEM, ANY],
        out_specs=[ANY] * 5,
        out_shape=[shaped((8, 2, 32, 256), F32)] + [shaped((2, 8, 32, 256), F32)] * 4,
        scratch_shapes=[
            VMEM((2, 256, 8, 256), F32),
            VMEM((256, 8, 256), F32),
            VMEM((9, 256, 256), F32),
            pltpu.SemaphoreType.DMA((40,)),
        ],
        compiler_params=params(58),
        name="pack_first",
    )(where, pattern, perm, matrix)


def pack_body(where_ref, pattern_ref, perm_ref, a_ref, after_ref, out0_ref, out1_ref, moved):
    for m, out_ref in enumerate((out0_ref, out1_ref)):
        gather_rows(m, perm_ref, a_ref.at[m], moved)
        for c in range(8):
            out_ref[c] = block_of(m, c, where_ref, pattern_ref, moved)


def pack(where, pattern, perm, matrix, after):
    return pl.pallas_call(
        pack_body,
        in_specs=[SMEM, SMEM, SMEM, HERE, ANY],
        out_specs=[HERE, HERE],
        out_shape=[shaped((8, 256, 256), F32)] * 2,
        scratch_shapes=[VMEM((256, 8, 256), F32)],
        compiler_params=params(20),
        name="pack",
    )(where, pattern, perm, matrix, after)


def hold_body(where_ref, own_ref, far0, far1, columns_ref, both_ref, sem):
    near = where_ref[3] < 4
    for h, far in enumerate((far0, far1)):
        here = pltpu.make_async_copy(own_ref.at[h], both_ref.at[h], sem.at[h])
        there = pltpu.make_async_copy(far, both_ref.at[h], sem.at[h])

        @pl.when(near)
        def _():
            here.start()

        @pl.when(jnp.logical_not(near))
        def _():
            there.start()

    for h in range(2):
        pltpu.make_async_copy(own_ref.at[h], both_ref.at[h], sem.at[h]).wait()


def hold(where, own, far, columns):
    return pl.pallas_call(
        hold_body,
        in_specs=[SMEM] + [HERE] * 3 + [ANY],
        out_specs=HERE,
        out_shape=shaped((2, 9, 32, 256), F32),
        scratch_shapes=[pltpu.SemaphoreType.DMA((2,))],
        compiler_params=params(4),
        name="hold",
    )(where, own, far[0], far[1], columns)


def merge_body(
    found_ref, held, after, before, two,
    all_ref, half0, half1, corner_ref, stage, slices, sem,
):
    pieces = [(r, h) for r in range(3) for h in range(2)]
    arrive = []
    for n, (r, h) in enumerate(pieces):
        found = found_ref[n]

        def load(part, n=n, r=r, h=h):
            return pltpu.make_async_copy(part.at[h], stage.at[h, r], sem.at[n])

        for which, part in enumerate((held, after, before, two)):

            @pl.when(found == which)
            def _():
                load(part).start()

        arrive.append(load(held))
    eight = pl.ds(0, 8)
    small, last = [], []
    for n, (r, h) in enumerate(pieces):
        arrive[n].wait()
        k = 6 + 3 * n
        last.append(pltpu.make_async_copy(stage.at[h, r, eight], all_ref.at[h, r], sem.at[k]))
        last.append(
            pltpu.make_async_copy(stage.at[h, r, eight], (half0, half1)[h].at[r], sem.at[k + 1])
        )
        small.append(pltpu.make_async_copy(stage.at[h, r, 8], slices.at[r, h], sem.at[k + 2]))
        last[-2].start()
        last[-1].start()
        small[-1].start()
    for one in small:
        one.wait()
    for q in range(8):
        last.append(pltpu.make_async_copy(slices, corner_ref.at[q], sem.at[24 + q]))
        last[-1].start()
    for one in last:
        one.wait()


def merge(found, *parts):
    half = shaped((3, 8, 32, 256), F32)
    return pl.pallas_call(
        merge_body,
        in_specs=[SMEM] + [ANY] * 4,
        out_specs=[ANY] * 4,
        out_shape=[
            shaped((2, 3, 8, 32, 256), F32), half, half, shaped((8, 3, 2, 32, 256), F32)
        ],
        scratch_shapes=[
            VMEM((2, 3, 9, 32, 256), F32),
            VMEM((3, 2, 32, 256), F32),
            pltpu.SemaphoreType.DMA((32,)),
        ],
        compiler_params=params(58),
        name="merge",
    )(found, *parts)


def left_body(
    where_ref, pattern_ref, columns_ref, corner_ref, linv_ref, uinv_ref,
    ll_ref, c3_ref, li_ref, raw_ref, column, both, linv, uinv, sem,
):
    prow = where_ref[0]
    copies = [
        pltpu.make_async_copy(linv_ref, linv, sem.at[0]),
        pltpu.make_async_copy(uinv_ref, uinv, sem.at[1]),
    ]
    for q in range(8):
        rows = pl.ds(q * 32, 32)
        copies.append(pltpu.make_async_copy(corner_ref.at[q], both.at[:, :, rows], sem.at[2 + q]))
        copies.append(pltpu.make_async_copy(columns_ref.at[q], column.at[:, :, rows], sem.at[10 + q]))
    for one in copies:
        one.start()
    for one in copies:
        one.wait()
    li = [wide(linv[k]) for k in range(3)]
    ui = [tall(uinv[k]) for k in range(3)]
    for k in range(3):
        li_ref[k] = li[k]
    a01, a02 = both[0, 0], both[0, 1]
    a10, a12 = both[1, 0], both[1, 1]
    a20, a21 = both[2, 0], both[2, 1]
    u01 = tall(dot(li[0], tall(a01)))
    u02 = tall(dot(li[0], tall(a02)))
    l10 = wide(dot(wide(a10), ui[0]))
    l20 = wide(dot(wide(a20), ui[0]))
    p12 = pattern_ref[1, 2].astype(F32)
    p21 = pattern_ref[2, 1].astype(F32)
    u12 = tall(dot(li[1], tall(a12 - p12 * dot(l10, u02))))
    l21 = wide(dot(wide(a21 - p21 * dot(l20, u01)), ui[1]))
    for n, value in enumerate((l10, l20, l21)):
        c3_ref[n] = value
    for m in range(2):
        row = m * 32 + prow
        rows = pl.ds(m * 256, 256)
        l0 = dot(wide(column[0, m]), ui[0])
        l0w = wide(l0)
        p1 = pattern_ref[row, 1].astype(F32)
        l1 = dot(wide(column[1, m] - p1 * dot(l0w, u01)), ui[1])
        l1w = wide(l1)
        p2 = pattern_ref[row, 2].astype(F32)
        l2 = dot(wide(column[2, m] - p2 * (dot(l0w, u02) + dot(l1w, u12))), ui[2])
        for k, value in enumerate((l0, l1, l2)):
            raw_ref[k, m] = value
            high, low = split(jnp.where(row > k, value, 0.0))
            ll_ref[rows, pl.ds(k * 768, 256)] = high
            ll_ref[rows, pl.ds(k * 768 + 256, 256)] = high
            ll_ref[rows, pl.ds(k * 768 + 512, 256)] = low


def left(where, pattern, columns, corner, lower_inv, upper_inv):
    outs = [
        shaped((512, 2304), BF16),
        shaped((3, 256, 768), BF16),
        shaped((3, 256, 768), BF16),
        shaped((3, 2, 256, 256), F32),
    ]
    return pl.pallas_call(
        left_body,
        in_specs=[SMEM, SMEM, ANY, ANY, ANY, ANY],
        out_specs=[HERE] * 4,
        out_shape=outs,
        scratch_shapes=[
            VMEM((3, 2, 256, 256), F32),
            VMEM((3, 2, 256, 256), F32),
            VMEM((3, 256, 256), F32),
            VMEM((3, 256, 256), F32),
            pltpu.SemaphoreType.DMA((18,)),
        ],
        compiler_params=params(20),
        name="left",
    )(where, pattern, columns, corner, lower_inv, upper_inv)


RANGES = ((0, 4), (4, 8))


def finish_body(
    where_ref, pattern_ref, ap0, ap1, ll, c3, li, raw, mine, lower, higher, half0, half1,
    out_ref, panel, upper, out, sem,
):
    prow, pcol, turn = where_ref[0], where_ref[1], where_ref[2]
    count = [0]

    def copy(source, target):
        one = pltpu.make_async_copy(source, target, sem.at[count[0]])
        count[0] += 1
        one.start()
        return one

    starts = [pl.multiple_of(lax.rem(turn + s, 4) * 64, 64) for s in SHIFTS]
    halves = [ref.at[h] for ref in (mine, lower, higher) for h in range(2)] + [half0, half1]

    def panels(n):
        lo, hi = RANGES[n]
        part = pl.ds(lo, hi - lo)
        for slot in range(4):
            for h in range(2):
                rows = pl.ds(starts[slot] + h * 32, 32)
                yield copy(halves[slot * 2 + h].at[:, part], panel.at[:, part, rows])

    def wait(group):
        for one in group:
            one.wait()

    def keep(i, c):
        return pattern_ref[i, c * 8 + pcol].astype(F32)

    def keeps(k, group):
        return jnp.concatenate([jnp.full((1, 256), keep(k, c), F32) for c in group], axis=1)

    def block(k, group):
        return jnp.concatenate([panel[k, c] for c in group], axis=1)

    def done(k, group, value):
        for n, c in enumerate(group):
            panel[k, c] = value[:, n * 256 : (n + 1) * 256]
        value = tall(value)
        upper[pl.ds(k * 768, 768), pl.ds(group[0] * 256, len(group) * 256)] = value
        return value

    def stages(group):
        u0 = done(0, group, dot(li[0], tall(block(0, group))))
        yield
        both = dot(c3[pl.ds(0, 2)].reshape(512, 768), u0)
        value = block(1, group) - keeps(1, group) * both[:256]
        u1 = done(1, group, dot(li[1], tall(value)))
        yield
        both = both[256:] + dot(c3[2], u1)
        value = block(2, group) - keeps(2, group) * both
        done(2, group, dot(li[2], tall(value)))
        yield

    def fix(m):
        @pl.when(jnp.logical_and(pcol < 3, m * 32 + prow > pcol))
        def _():
            out[m, :, 0, :] = raw[jnp.minimum(pcol, 2), m]

        if m == 0:

            @pl.when(prow < 3)
            def _():
                mine = jnp.minimum(prow, 2)
                for c in range(8):

                    @pl.when(prow < c * 8 + pcol)
                    def _():
                        out[0, :, c, :] = panel[mine, c]

    def update(c, m):
        total = dot(ll[pl.ds(m * 256, 256), :], upper[:, pl.ds(c * 256, 256)])
        out[m, :, c, :] = (ap0, ap1)[m][c] - keep(m * 32 + prow, c) * total

    groups = [[*panels(n)] for n in range(2)]
    wait(groups[0])
    for _ in stages(range(4)):
        pass
    wait(groups[1])
    for n, _ in enumerate(stages(range(4, 8))):
        if n < 2:
            for c in range(4):
                update(c, n)
    for c in range(4, 8):
        update(c, 0)
    fix(0)
    last = [copy(out.at[0], out_ref.at[0])]
    for c in (4, 5, 6, 7):
        update(c, 1)
    fix(1)
    last.append(copy(out.at[1], out_ref.at[1]))
    wait(last)


def finish(where, pattern, ap0, ap1, ll, c3, li, raw, *mains):
    return pl.pallas_call(
        finish_body,
        in_specs=[SMEM, SMEM] + [HERE] * 6 + [ANY] * 5,
        out_specs=ANY,
        out_shape=shaped((2, 256, 8, 256), F32),
        scratch_shapes=[
            VMEM((3, 8, 256, 256), F32),
            VMEM((2304, 2048), BF16),
            VMEM((2, 256, 8, 256), F32),
            pltpu.SemaphoreType.DMA((48,)),
        ],
        compiler_params=params(28),
        name="finish",
    )(where, pattern, ap0, ap1, ll, c3, li, raw, *mains)


def hop(array, steps, sources=lambda x, z: True):
    pairs = []
    for x in range(NX):
        for z in range(NZ):
            if sources(x, z):
                step = steps[z] if len(steps) > 1 else steps[0]
                to = ((x + step[0]) % NX) * NZ + (z + step[1]) % NZ
                pairs.append((x * NZ + z, to))
    return lax.ppermute(array, "prow", pairs)


def to_all(array):
    count = lax.axis_size("pcol")
    return lax.all_to_all(jnp.broadcast_to(array, (count, *array.shape)), "pcol", 0, 0)


PICK = (
    ((0, 1, 3, 2, 0, 1, 3, 2), (0, 1, 3, 2, 0, 1, 3, 2)),
    ((2, 0, 1, 3, 2, 0, 1, 3), (2, 0, 1, 3, 2, 0, 1, 3)),
    ((3, 2, 0, 1, 3, 2, 0, 1), (1, 2, 0, 1, 3, 3, 2, 0)),
)


def on_device(matrix, pattern, row_perm, lower_inv, upper_inv):
    prow = lax.axis_index("prow")
    pcol = lax.axis_index("pcol")
    x, z = prow // NZ, prow % NZ
    root = lambda x, z: x == 0 and z < 3
    where = jnp.stack([prow, pcol, lax.rem(x + 2 * z, 4), z]).astype(jnp.int32)
    faces, *cut = pack_first(where, pattern, row_perm, matrix)
    sent = [hop(cut[d], [(d, 0)], root) for d in (2, 1, 3)]
    faces = lax.all_to_all(faces, "pcol", 0, 0)
    columns = to_all(faces[:3])
    extra = jnp.stack(
        [jnp.where(z == 0, faces[1, 0], faces[0, 0]), jnp.where(z == 2, faces[1, 0], faces[2, 0])]
    )
    extra_sent = [hop(extra, [(d, 0)], root) for d in (2, 1, 3)]
    own = jnp.where(x == 0, cut[0], sum(sent))
    own_extra = jnp.where(x == 0, extra, sum(extra_sent))
    own = jnp.concatenate([own, own_extra[:, None]], axis=1)
    far = [
        hop(own[0], [(0, 4)], lambda x, z: z < 3),
        hop(own[1], [(0, 4), (0, 4), (2, 5)], lambda x, z: z < 3),
    ]
    both = hold(where, own, far, columns)
    after = hop(both, [(2, 1)], lambda x, z: z != 3)
    before = hop(both, [(2, -1)], lambda x, z: z != 3)
    steps = [(0, 2), (0, -2), (0, 2), None, (0, 2), (0, -2), (0, 2), (0, -2)]
    two = hop(both, steps, lambda x, z: z != 3)
    found = jnp.array(PICK, jnp.int32)[:, :, z].reshape(6)
    mine, half0, half1, corner = merge(found, both, after, before, two)
    corner = lax.all_to_all(corner, "pcol", 0, 0)
    ap0, ap1 = pack(where, pattern, row_perm, matrix, mine)
    lower, higher = hop(mine, [(1, 0)]), hop(mine, [(-1, 0)])
    half0, half1 = hop(half0, [(0, 1)]), hop(half1, [(0, -1)])
    ll, c3, li, raw = left(where, pattern, columns, corner, lower_inv, upper_inv)
    return finish(where, pattern, ap0, ap1, ll, c3, li, raw, mine, lower, higher, half0, half1)


def solution(mesh):
    P = jax.sharding.PartitionSpec
    in_specs = (P(None, "prow", None, "pcol"), P(), P(None, "prow"), P(), P())
    out_specs = P(None, "prow", None, "pcol")
    return jax.shard_map(
        on_device, mesh=mesh, in_specs=in_specs, out_specs=out_specs, check_vma=False
    )
```

```python
import functools

import jax
import jax.numpy as jnp
from jax import lax
from jax.experimental import pallas as pl
from jax.experimental.pallas import tpu as pltpu

NX, NZ = 4, 8
SHIFTS = (0, 3, 1, 2)
SMEM = pl.BlockSpec(memory_space=pltpu.SMEM)
ANY = pl.BlockSpec(memory_space=pl.ANY)
HERE = pl.BlockSpec(memory_space=pltpu.VMEM)
VMEM = pltpu.VMEM
F32 = jnp.float32
BF16 = jnp.bfloat16
shaped = jax.ShapeDtypeStruct


def params(mib):
    return pltpu.CompilerParams(vmem_limit_bytes=mib * 2**20)


def split(value):
    high = value.astype(BF16)
    return high, (value - high.astype(F32)).astype(BF16)


def wide(value):
    high, low = split(value)
    return jnp.concatenate([high, high, low], axis=1)


def tall(value):
    high, low = split(value)
    return jnp.concatenate([high, low, high], axis=0)


def dot(a, b):
    return jnp.dot(a, b, preferred_element_type=F32)


def gather_rows(m, perm_ref, source, moved):
    def move(r, carry):
        for u in range(16):
            moved[r * 16 + u] = source[perm_ref[m, r * 16 + u]]
        return carry

    lax.fori_loop(0, 16, move, 0)


def block_of(m, c, where_ref, pattern_ref, moved):
    keep = pattern_ref[m * 32 + where_ref[0], c * 8 + where_ref[1]].astype(F32)
    return moved[:, c, :] * keep


def pack_first_body(
    where_ref, pattern_ref, perm_ref, a_ref, faces_ref, m0, m1, m2, m3, raw, moved, packed, sem,
):
    loads = [
        pltpu.make_async_copy(
            a_ref.at[m, pl.ds(n * 64, 64)], raw.at[m, pl.ds(n * 64, 64)], sem.at[m * 4 + n]
        )
        for m in range(2)
        for n in range(4)
    ]
    for load in loads:
        load.start()
    for load in loads[:4]:
        load.wait()
    gather_rows(0, perm_ref, raw.at[0], moved)
    copies = []

    def copy(source, target):
        one = pltpu.make_async_copy(source, target, sem.at[8 + len(copies)])
        one.start()
        copies.append(one)

    def face(m, block):
        for j in range(8):
            copy(packed.at[block, pl.ds(j * 32, 32)], faces_ref.at[j, m])

    mains = (m0, m1, m2, m3)
    turn = where_ref[2]
    starts = [pl.multiple_of(lax.rem(turn + slot, 4) * 64, 64) for slot in range(4)]
    for c in range(8):
        packed[c] = block_of(0, c, where_ref, pattern_ref, moved)
        if c == 0:
            face(0, 0)
        if c % 4 == 3:
            part = pl.ds(c - 3, 4)
            for slot in (2, 1, 3, 0):
                for h in range(2):
                    rows = pl.ds(starts[slot] + h * 32, 32)
                    copy(packed.at[part, rows], mains[slot].at[h, part])
    for load in loads[4:]:
        load.wait()
    gather_rows(1, perm_ref, raw.at[1], moved)
    packed[8] = block_of(1, 0, where_ref, pattern_ref, moved)
    face(1, 8)
    for one in copies:
        one.wait()


def pack_first(where, pattern, perm, matrix):
    return pl.pallas_call(
        pack_first_body,
        in_specs=[SMEM, SMEM, SMEM, ANY],
        out_specs=[ANY] * 5,
        out_shape=[shaped((8, 2, 32, 256), F32)] + [shaped((2, 8, 32, 256), F32)] * 4,
        scratch_shapes=[
            VMEM((2, 256, 8, 256), F32),
            VMEM((256, 8, 256), F32),
            VMEM((9, 256, 256), F32),
            pltpu.SemaphoreType.DMA((40,)),
        ],
        compiler_params=params(58),
        name="pack_first",
    )(where, pattern, perm, matrix)


def pack_body(where_ref, pattern_ref, perm_ref, a_ref, after_ref, out0_ref, out1_ref, moved):
    for m, out_ref in enumerate((out0_ref, out1_ref)):
        gather_rows(m, perm_ref, a_ref.at[m], moved)
        for c in range(8):
            out_ref[c] = block_of(m, c, where_ref, pattern_ref, moved)


def pack(where, pattern, perm, matrix, after):
    return pl.pallas_call(
        pack_body,
        in_specs=[SMEM, SMEM, SMEM, HERE, ANY],
        out_specs=[HERE, HERE],
        out_shape=[shaped((8, 256, 256), F32)] * 2,
        scratch_shapes=[VMEM((256, 8, 256), F32)],
        compiler_params=params(20),
        name="pack",
    )(where, pattern, perm, matrix, after)


def hold_body(where_ref, own_ref, far0, far1, columns_ref, both_ref, sem):
    near = where_ref[3] < 4
    for h, far in enumerate((far0, far1)):
        here = pltpu.make_async_copy(own_ref.at[h], both_ref.at[h], sem.at[h])
        there = pltpu.make_async_copy(far, both_ref.at[h], sem.at[h])

        @pl.when(near)
        def _():
            here.start()

        @pl.when(jnp.logical_not(near))
        def _():
            there.start()

    for h in range(2):
        pltpu.make_async_copy(own_ref.at[h], both_ref.at[h], sem.at[h]).wait()


def hold(where, own, far, columns):
    return pl.pallas_call(
        hold_body,
        in_specs=[SMEM] + [HERE] * 3 + [ANY],
        out_specs=HERE,
        out_shape=shaped((2, 9, 32, 256), F32),
        scratch_shapes=[pltpu.SemaphoreType.DMA((2,))],
        compiler_params=params(4),
        name="hold",
    )(where, own, far[0], far[1], columns)


def merge_body(
    found_ref, held, after, before, two,
    all_ref, corner_ref, stage, slices, sem,
):
    pieces = [(r, h) for r in range(3) for h in range(2)]
    arrive = []
    for n, (r, h) in enumerate(pieces):
        found = found_ref[n]

        def load(part, n=n, r=r, h=h):
            return pltpu.make_async_copy(part.at[h], stage.at[h, r], sem.at[n])

        for which, part in enumerate((held, after, before, two)):

            @pl.when(found == which)
            def _():
                load(part).start()

        arrive.append(load(held))
    eight = pl.ds(0, 8)
    small, last = [], []
    for n, (r, h) in enumerate(pieces):
        arrive[n].wait()
        last.append(
            pltpu.make_async_copy(stage.at[h, r, eight], all_ref.at[h, r], sem.at[6 + 2 * n])
        )
        small.append(pltpu.make_async_copy(stage.at[h, r, 8], slices.at[r, h], sem.at[7 + 2 * n]))
        last[-1].start()
        small[-1].start()
    for one in small:
        one.wait()
    for q in range(8):
        last.append(pltpu.make_async_copy(slices, corner_ref.at[q], sem.at[18 + q]))
        last[-1].start()
    for one in last:
        one.wait()


def merge(found, *parts):
    return pl.pallas_call(
        merge_body,
        in_specs=[SMEM] + [ANY] * 4,
        out_specs=[ANY] * 2,
        out_shape=[shaped((2, 3, 8, 32, 256), F32), shaped((8, 3, 2, 32, 256), F32)],
        scratch_shapes=[
            VMEM((2, 3, 9, 32, 256), F32),
            VMEM((3, 2, 32, 256), F32),
            pltpu.SemaphoreType.DMA((26,)),
        ],
        compiler_params=params(58),
        name="merge",
    )(found, *parts)


def left_body(
    where_ref, pattern_ref, columns_ref, corner_ref, linv_ref, uinv_ref,
    ll_ref, c3_ref, li_ref, raw_ref, column, both, linv, uinv, sem,
):
    prow = where_ref[0]
    copies = [
        pltpu.make_async_copy(linv_ref, linv, sem.at[0]),
        pltpu.make_async_copy(uinv_ref, uinv, sem.at[1]),
    ]
    for q in range(8):
        rows = pl.ds(q * 32, 32)
        copies.append(pltpu.make_async_copy(corner_ref.at[q], both.at[:, :, rows], sem.at[2 + q]))
        copies.append(pltpu.make_async_copy(columns_ref.at[q], column.at[:, :, rows], sem.at[10 + q]))
    for one in copies:
        one.start()
    for one in copies:
        one.wait()
    li = [wide(linv[k]) for k in range(3)]
    ui = [tall(uinv[k]) for k in range(3)]
    for k in range(3):
        li_ref[k] = li[k]
    a01, a02 = both[0, 0], both[0, 1]
    a10, a12 = both[1, 0], both[1, 1]
    a20, a21 = both[2, 0], both[2, 1]
    u01 = tall(dot(li[0], tall(a01)))
    u02 = tall(dot(li[0], tall(a02)))
    l10 = wide(dot(wide(a10), ui[0]))
    l20 = wide(dot(wide(a20), ui[0]))
    p12 = pattern_ref[1, 2].astype(F32)
    p21 = pattern_ref[2, 1].astype(F32)
    u12 = tall(dot(li[1], tall(a12 - p12 * dot(l10, u02))))
    l21 = wide(dot(wide(a21 - p21 * dot(l20, u01)), ui[1]))
    for n, value in enumerate((l10, l20, l21)):
        c3_ref[n] = value
    for m in range(2):
        row = m * 32 + prow
        rows = pl.ds(m * 256, 256)
        l0 = dot(wide(column[0, m]), ui[0])
        l0w = wide(l0)
        p1 = pattern_ref[row, 1].astype(F32)
        l1 = dot(wide(column[1, m] - p1 * dot(l0w, u01)), ui[1])
        l1w = wide(l1)
        p2 = pattern_ref[row, 2].astype(F32)
        l2 = dot(wide(column[2, m] - p2 * (dot(l0w, u02) + dot(l1w, u12))), ui[2])
        for k, value in enumerate((l0, l1, l2)):
            raw_ref[k, m] = value
            high, low = split(jnp.where(row > k, value, 0.0))
            ll_ref[rows, pl.ds(k * 768, 256)] = high
            ll_ref[rows, pl.ds(k * 768 + 256, 256)] = high
            ll_ref[rows, pl.ds(k * 768 + 512, 256)] = low


def left(where, pattern, columns, corner, lower_inv, upper_inv):
    outs = [
        shaped((512, 2304), BF16),
        shaped((3, 256, 768), BF16),
        shaped((3, 256, 768), BF16),
        shaped((3, 2, 256, 256), F32),
    ]
    return pl.pallas_call(
        left_body,
        in_specs=[SMEM, SMEM, ANY, ANY, ANY, ANY],
        out_specs=[HERE] * 4,
        out_shape=outs,
        scratch_shapes=[
            VMEM((3, 2, 256, 256), F32),
            VMEM((3, 2, 256, 256), F32),
            VMEM((3, 256, 256), F32),
            VMEM((3, 256, 256), F32),
            pltpu.SemaphoreType.DMA((18,)),
        ],
        compiler_params=params(20),
        name="left",
    )(where, pattern, columns, corner, lower_inv, upper_inv)


RANGES = ((0, 4), (4, 8))


def finish_body(
    where_ref, pattern_ref, ap0, ap1, ll, c3, li, raw, mine, lower, higher, below,
    out_ref, panel, upper, out, sem,
):
    prow, pcol, turn = where_ref[0], where_ref[1], where_ref[2]
    count = [0]

    def copy(source, target):
        one = pltpu.make_async_copy(source, target, sem.at[count[0]])
        count[0] += 1
        one.start()
        return one

    starts = [pl.multiple_of(lax.rem(turn + s, 4) * 64, 64) for s in SHIFTS]
    halves = [ref.at[h] for ref in (mine, lower, higher, below) for h in range(2)]

    def panels(n):
        lo, hi = RANGES[n]
        part = pl.ds(lo, hi - lo)
        for slot in range(4):
            for h in range(2):
                rows = pl.ds(starts[slot] + h * 32, 32)
                yield copy(halves[slot * 2 + h].at[:, part], panel.at[:, part, rows])

    def wait(group):
        for one in group:
            one.wait()

    def keep(i, c):
        return pattern_ref[i, c * 8 + pcol].astype(F32)

    def keeps(k, group):
        return jnp.concatenate([jnp.full((1, 256), keep(k, c), F32) for c in group], axis=1)

    def block(k, group):
        return jnp.concatenate([panel[k, c] for c in group], axis=1)

    def done(k, group, value):
        for n, c in enumerate(group):
            panel[k, c] = value[:, n * 256 : (n + 1) * 256]
        value = tall(value)
        upper[pl.ds(k * 768, 768), pl.ds(group[0] * 256, len(group) * 256)] = value
        return value

    def stages(group):
        u0 = done(0, group, dot(li[0], tall(block(0, group))))
        yield
        both = dot(c3[pl.ds(0, 2)].reshape(512, 768), u0)
        value = block(1, group) - keeps(1, group) * both[:256]
        u1 = done(1, group, dot(li[1], tall(value)))
        yield
        both = both[256:] + dot(c3[2], u1)
        value = block(2, group) - keeps(2, group) * both
        done(2, group, dot(li[2], tall(value)))
        yield

    def fix(m):
        @pl.when(jnp.logical_and(pcol < 3, m * 32 + prow > pcol))
        def _():
            out[m, :, 0, :] = raw[jnp.minimum(pcol, 2), m]

        if m == 0:

            @pl.when(prow < 3)
            def _():
                mine = jnp.minimum(prow, 2)
                for c in range(8):

                    @pl.when(prow < c * 8 + pcol)
                    def _():
                        out[0, :, c, :] = panel[mine, c]

    def update(c, m):
        total = dot(ll[pl.ds(m * 256, 256), :], upper[:, pl.ds(c * 256, 256)])
        out[m, :, c, :] = (ap0, ap1)[m][c] - keep(m * 32 + prow, c) * total

    groups = [[*panels(n)] for n in range(2)]
    wait(groups[0])
    for _ in stages(range(4)):
        pass
    wait(groups[1])
    for n, _ in enumerate(stages(range(4, 8))):
        if n < 2:
            for c in range(4):
                update(c, n)
    for c in range(4, 8):
        update(c, 0)
    fix(0)
    last = [copy(out.at[0], out_ref.at[0])]
    for c in (4, 5, 6, 7):
        update(c, 1)
    fix(1)
    last.append(copy(out.at[1], out_ref.at[1]))
    wait(last)


def finish(where, pattern, ap0, ap1, ll, c3, li, raw, *mains):
    return pl.pallas_call(
        finish_body,
        in_specs=[SMEM, SMEM] + [HERE] * 6 + [ANY] * 4,
        out_specs=ANY,
        out_shape=shaped((2, 256, 8, 256), F32),
        scratch_shapes=[
            VMEM((3, 8, 256, 256), F32),
            VMEM((2304, 2048), BF16),
            VMEM((2, 256, 8, 256), F32),
            pltpu.SemaphoreType.DMA((48,)),
        ],
        compiler_params=params(28),
        name="finish",
    )(where, pattern, ap0, ap1, ll, c3, li, raw, *mains)


def hop(array, steps, sources=lambda x, z: True):
    pairs = []
    for x in range(NX):
        for z in range(NZ):
            if sources(x, z):
                step = steps[z] if len(steps) > 1 else steps[0]
                to = ((x + step[0]) % NX) * NZ + (z + step[1]) % NZ
                pairs.append((x * NZ + z, to))
    return lax.ppermute(array, "prow", pairs)


def to_all(array):
    count = lax.axis_size("pcol")
    return lax.all_to_all(jnp.broadcast_to(array, (count, *array.shape)), "pcol", 0, 0)


PICK = (
    ((0, 1, 3, 2, 0, 1, 3, 2), (0, 1, 3, 2, 0, 1, 3, 2)),
    ((2, 0, 1, 3, 2, 0, 1, 3), (2, 0, 1, 3, 2, 0, 1, 3)),
    ((3, 2, 0, 1, 3, 2, 0, 1), (1, 2, 0, 1, 3, 3, 2, 0)),
)


def on_device(matrix, pattern, row_perm, lower_inv, upper_inv):
    prow = lax.axis_index("prow")
    pcol = lax.axis_index("pcol")
    x, z = prow // NZ, prow % NZ
    root = lambda x, z: x == 0 and z < 3
    where = jnp.stack([prow, pcol, lax.rem(x + 2 * z, 4), z]).astype(jnp.int32)
    faces, *cut = pack_first(where, pattern, row_perm, matrix)
    sent = [hop(cut[d], [(d, 0)], root) for d in (2, 1, 3)]
    faces = lax.all_to_all(faces, "pcol", 0, 0)
    columns = to_all(faces[:3])
    extra = jnp.stack(
        [jnp.where(z == 0, faces[1, 0], faces[0, 0]), jnp.where(z == 2, faces[1, 0], faces[2, 0])]
    )
    extra_sent = [hop(extra, [(d, 0)], root) for d in (2, 1, 3)]
    own = jnp.where(x == 0, cut[0], sum(sent))
    own_extra = jnp.where(x == 0, extra, sum(extra_sent))
    own = jnp.concatenate([own, own_extra[:, None]], axis=1)
    far = [
        hop(own[0], [(0, 4)], lambda x, z: z < 3),
        hop(own[1], [(0, 4), (0, 4), (2, 5)], lambda x, z: z < 3),
    ]
    both = hold(where, own, far, columns)
    after = hop(both, [(2, 1)], lambda x, z: z != 3)
    before = hop(both, [(2, -1)], lambda x, z: z != 3)
    steps = [(0, 2), (0, -2), (0, 2), None, (0, 2), (0, -2), (0, 2), (0, -2)]
    two = hop(both, steps, lambda x, z: z != 3)
    found = jnp.array(PICK, jnp.int32)[:, :, z].reshape(6)
    mine, corner = merge(found, both, after, before, two)
    corner = lax.all_to_all(corner, "pcol", 0, 0)
    ap0, ap1 = pack(where, pattern, row_perm, matrix, mine)
    lower, higher = hop(mine, [(1, 0)]), hop(mine, [(-1, 0)])
    below = hop(mine, [(0, 1)])
    ll, c3, li, raw = left(where, pattern, columns, corner, lower_inv, upper_inv)
    return finish(where, pattern, ap0, ap1, ll, c3, li, raw, mine, lower, higher, below)


def solution(mesh):
    P = jax.sharding.PartitionSpec
    in_specs = (P(None, "prow", None, "pcol"), P(), P(None, "prow"), P(), P())
    out_specs = P(None, "prow", None, "pcol")
    return jax.shard_map(
        on_device, mesh=mesh, in_specs=in_specs, out_specs=out_specs, check_vma=False
    )
```
